256 devices in a mesh: section: 16 (over z, x_hi), dp: 16 (over x_lo, y, core).
Axes of the slice: x: 4 (x_hi: 2, x_lo: 2; x = x_hi * 2 + x_lo), y: 4, z: 8, core: 2. Of those that a mesh axis runs over, the one named last changes fastest.
Arguments:
- section_input: bfloat16 [16, 2048, 12288], P('section', 'dp'), may hold values from -0.19921875 to 0.19921875
- boundary_grad: bfloat16 [16, 2048, 12288], P('section', 'dp'), may hold values from -6 to 6
- carry_error: bfloat16 [16, 2048, 12288], P('section', 'dp'), may hold values from -4 to 4
- act_basis: bfloat16 [16, 12288, 64], P('section', 'dp'), may hold values from -6 to 6
- weight_basis: bfloat16 [16, 12288, 128], P('section', 'dp'), may hold values from -6 to 6
- outside_left: bfloat16 [2048, 64], P('dp'), may hold values from -1 to 1
- outside_right: bfloat16 [16, 12288, 64], P('dp', 'section'), may hold values from -6 to 6
Outputs:
- new_error: bfloat16 [16, 2048, 12288], P('section', 'dp')
- weight_left: bfloat16 [16, 12288, 128], P('section', 'dp')
- weight_right: bfloat16 [16, 12288, 128], P('section', 'dp')
The draws below stay inside these ranges and needn't reach their ends.
All inputs are finite; a program needn't handle non-finite values.
Results may differ from the reference program's by a relative error of at most 0.03.
Values may be sent and summed in bfloat16 or wider, within the bound.
No kernel may reach another device: no remote copies, remote signals or barrier semaphores. Data moves between devices by JAX's collectives and lax.ppermute only.
A program may use at most 64 MiB of HBM per device.

```python
import jax
import jax.numpy as jnp
from jax import lax

D = 12288
RA = 64
RW = 128
ROWS = 128
TOKENS = 2048
SECTIONS = 16
N_SECTION = 16
N_DP = 16


def steps_of(stream_key, extent, pieces, low, top_value):
    def one(axis_at, shards_of):
        heights = jax.random.uniform(jax.random.fold_in(jax.random.fold_in(stream_key, 6), axis_at), (shards_of,), jnp.float32, low / len(pieces), top_value / len(pieces))
        return jnp.repeat(jnp.exp(heights), extent[axis_at] // shards_of).reshape((-1,) + (1,) * (len(extent) - axis_at - 1))

    level = one(*pieces[0])
    for cut in pieces[1:]:
        level = level * one(*cut)
    return level


def normal_values(key, shape, spread, reach, shards=(), kind=jnp.bfloat16):
    result = spread * jax.random.normal(key, shape, jnp.float32)
    if shards:
        result = result * steps_of(key, shape, shards, -0.22, 0.18)
    return jnp.clip(result, -reach, reach).astype(kind)


def setup_inputs(seed: int = 0) -> dict:
    splits = jax.random.split(jax.random.key(seed), 8)
    section_input = normal_values(splits[0], (SECTIONS, TOKENS, D), 0.03, 0.19921875, ((0, 16), (1, 16)))
    boundary_grad = normal_values(splits[1], (SECTIONS, TOKENS, D), 1.0, 6.0, ((0, 16), (1, 16)))
    carry_error = normal_values(splits[2], (SECTIONS, TOKENS, D), 0.5, 4.0, ((0, 16), (1, 16)))
    act_basis = normal_values(splits[3], (SECTIONS, D, RA), 1.0, 6.0, ((0, 16), (1, 16)))
    weight_basis = normal_values(splits[4], (SECTIONS, D, RW), 1.0, 6.0, ((0, 16), (1, 16)))
    outside_left = normal_values(splits[5], (TOKENS, RA), 0.125, 1.0, ((0, 16),))
    outside_right = normal_values(splits[6], (N_DP, D, RA), 1.0, 6.0, ((0, 16), (1, 16)))
    return {"section_input": section_input, "boundary_grad": boundary_grad, "carry_error": carry_error, "act_basis": act_basis, "weight_basis": weight_basis, "outside_left": outside_left, "outside_right": outside_right}


def orthonormal(block):
    gram = jnp.dot(block.T.astype(jnp.float32), block.astype(jnp.float32), precision=lax.Precision.HIGHEST, preferred_element_type=jnp.float32)
    factor = jnp.linalg.cholesky(gram)
    return jax.scipy.linalg.solve_triangular(factor, block.T, lower=True).T

def act_part(grad, error, basis):
    merged = grad.astype(jnp.float32) + error.astype(jnp.float32)
    proj = jnp.dot(merged, basis.astype(jnp.float32), precision=lax.Precision.HIGHEST)
    left = orthonormal(proj).astype(jnp.bfloat16)
    right = jnp.dot(merged.T, left.astype(jnp.float32), precision=lax.Precision.HIGHEST).astype(jnp.bfloat16)
    rebuilt = jnp.dot(left.astype(jnp.float32), right.T.astype(jnp.float32), preferred_element_type=jnp.float32)
    return (left, right, (merged - rebuilt).astype(jnp.bfloat16))

def left_term(inputs, left, right, basis):
    inner = jnp.dot(right.T.astype(jnp.float32), basis.astype(jnp.float32), preferred_element_type=jnp.float32).astype(jnp.bfloat16)
    core = jnp.dot(inputs.T.astype(jnp.float32), left.astype(jnp.float32), preferred_element_type=jnp.float32).astype(jnp.bfloat16)
    return jnp.dot(core.astype(jnp.float32), inner.astype(jnp.float32), preferred_element_type=jnp.float32).astype(jnp.bfloat16).astype(jnp.float32)

def right_term(inputs, left, right, factor):
    first = jnp.dot(inputs.astype(jnp.float32), factor.astype(jnp.float32), preferred_element_type=jnp.float32)
    middle = jnp.dot(left.astype(jnp.float32).T, first, precision=lax.Precision.HIGHEST).astype(jnp.bfloat16)
    return jnp.dot(right.astype(jnp.float32), middle.astype(jnp.float32), preferred_element_type=jnp.float32).astype(jnp.bfloat16).astype(jnp.float32)

def reference(section_input, boundary_grad, carry_error, act_basis, weight_basis, outside_left, outside_right):
    grads = boundary_grad.reshape(N_SECTION, N_DP, ROWS, D)
    errors = carry_error.reshape(N_SECTION, N_DP, ROWS, D)
    inputs = section_input.reshape(N_SECTION, N_DP, ROWS, D)

    def per_section(items):
        grad_s, error_s, basis_s = items
        return lax.map(lambda pair: act_part(pair[0], pair[1], basis_s), (grad_s, error_s))
    lefts, rights, errs = lax.map(per_section, (grads, errors, act_basis))
    recv_left = jnp.concatenate([lefts[1:], outside_left.reshape(1, N_DP, ROWS, RA)], axis=0)
    recv_right = jnp.concatenate([rights[1:], outside_right.reshape(1, N_DP, D, RA)], axis=0)

    def per_weight(items):
        input_s, left_s, right_s, basis_s = items
        terms = lax.map(lambda t: left_term(t[0], t[1], t[2], basis_s), (input_s, left_s, right_s))
        factor = orthonormal(jnp.sum(terms, axis=0)).astype(jnp.bfloat16)
        others = lax.map(lambda t: right_term(t[0], t[1], t[2], factor), (input_s, left_s, right_s))
        return (factor, jnp.sum(others, axis=0).astype(jnp.bfloat16))
    weight_left, weight_right = lax.map(per_weight, (inputs, recv_left, recv_right, weight_basis))
    return (errs.reshape(N_SECTION, N_DP * ROWS, D), weight_left, weight_right)
```

```python
import functools

import jax
import jax.numpy as jnp
from jax import lax
from jax.experimental import pallas as pl
from jax.experimental.pallas import tpu as pltpu
from jax.sharding import PartitionSpec as P

BF = jnp.bfloat16
F32 = jnp.float32
HIGHEST = lax.Precision.HIGHEST
VMEM_LIMIT = 48 * 1024 * 1024
PARAMS = pltpu.CompilerParams(vmem_limit_bytes=VMEM_LIMIT)
NN = (((1,), (0,)), ((), ()))
NT = (((1,), (1,)), ((), ()))
TN = (((0,), (0,)), ((), ()))


def dot(a, b, dims=NN, precision=None):
    return lax.dot_general(a, b, dims, precision=precision, preferred_element_type=F32)


def inverse_factor(gram):
    n = gram.shape[0]
    lane = lax.broadcasted_iota(jnp.int32, (1, n), 1)
    lane8 = lax.broadcasted_iota(jnp.int32, (8, n), 1)
    sub = lax.broadcasted_iota(jnp.int32, (8, n), 0)
    sub1 = lax.broadcasted_iota(jnp.int32, (8, 1), 0)
    work = gram
    done = []
    for first in range(0, n, 8):
        top = work[:8]
        rest = work[8:] if first + 8 < n else None
        for r in range(8):
            k = first + r
            pivot = top[r : r + 1, k : k + 1]
            scale = lax.rsqrt(pivot)
            scale = scale * (1.5 - 0.5 * pivot * scale * scale)
            row = jnp.where(lane == k, scale, top[r : r + 1, :] * scale)
            column = jnp.where(sub1 > r, top[:, k : k + 1] * scale, 0.0)
            cleared = jnp.where((lane8 == k) & (sub > r), 0.0, top)
            top = jnp.where(sub == r, row, cleared - column * row)
            if rest is not None:
                rest = jnp.where(lane == k, 0.0, rest) - (rest[:, k : k + 1] * scale) * row
        done.append(top)
        work = rest
    full = jnp.concatenate(done, axis=0)
    rows = lax.broadcasted_iota(jnp.int32, (n, n), 0)
    columns = lax.broadcasted_iota(jnp.int32, (n, n), 1)
    return jnp.where(columns <= rows, full, 0.0)


def proj_kernel(me_ref, g_ref, e_ref, own_ref, other_ref, left_ref, left_t_ref, acc):
    step = pl.program_id(0)
    width = own_ref.shape[1]
    core = lax.rem(me_ref[0], 2)
    mine = pl.ds(pl.multiple_of(core * width, width), width)
    others = pl.ds(pl.multiple_of((1 - core) * width, width), width)
    own, other = own_ref[...], other_ref[...]
    term = dot(g_ref[:, mine], own, NT) + dot(e_ref[:, mine], own, NT)
    term += dot(g_ref[:, others], other, NT) + dot(e_ref[:, others], other, NT)

    @pl.when(step == 0)
    def _():
        acc[...] = term

    @pl.when(step > 0)
    def _():
        acc[...] += term

    @pl.when(step == pl.num_programs(0) - 1)
    def _():
        proj = acc[...]
        inverse = inverse_factor(dot(proj, proj, TN, HIGHEST))
        left = dot(proj, inverse, NT, HIGHEST)
        left_ref[...] = left.astype(BF)
        left_t_ref[...] = left.T.astype(BF)


def act_left(me, grad, error, own, other):
    _, rows, width = grad.shape
    pieces, rank, part = own.shape
    pair = width // pieces
    wide = pl.BlockSpec((None, rows, pair), lambda m, me: (0, 0, (me[0] // 2) ^ m))
    narrow = pl.BlockSpec((None, rank, part), lambda m, me: (m, 0, 0))
    return pl.pallas_call(
        proj_kernel,
        grid_spec=pltpu.PrefetchScalarGridSpec(
            num_scalar_prefetch=1,
            grid=(pieces,),
            in_specs=[wide, wide, narrow, narrow],
            out_specs=[
                pl.BlockSpec((rows, rank), lambda m, me: (0, 0)),
                pl.BlockSpec((rank, rows), lambda m, me: (0, 0)),
            ],
            scratch_shapes=[pltpu.VMEM((rows, rank), F32)],
        ),
        out_shape=[jax.ShapeDtypeStruct((rows, rank), BF), jax.ShapeDtypeStruct((rank, rows), BF)],
        compiler_params=PARAMS,
    )(me, grad, error, own, other)


def right_kernel(g_ref, e_ref, left_ref, left_t_ref, error_ref, right_ref):
    g, e = g_ref[...], e_ref[...]
    left_t = left_t_ref[...]
    right = (dot(left_t, g) + dot(left_t, e)).astype(BF)
    rebuilt = dot(left_ref[...], right)
    error_ref[...] = (g.astype(F32) + e.astype(F32) - rebuilt).astype(BF)
    part = right_ref.shape[2]
    for i in range(right_ref.shape[0]):
        right_ref[i] = right[:, i * part : (i + 1) * part]


def act_right(grad, error, left, left_t, parts):
    _, rows, width = grad.shape
    rank = left_t.shape[0]
    steps = parts // 2
    wide = pl.BlockSpec((None, rows, width // steps), lambda m: (0, 0, m))
    return pl.pallas_call(
        right_kernel,
        grid=(steps,),
        in_specs=[
            wide,
            wide,
            pl.BlockSpec((rows, rank), lambda m: (0, 0)),
            pl.BlockSpec((rank, rows), lambda m: (0, 0)),
        ],
        out_specs=[wide, pl.BlockSpec((2, rank, width // parts), lambda m: (m, 0, 0))],
        out_shape=[
            jax.ShapeDtypeStruct(grad.shape, BF),
            jax.ShapeDtypeStruct((parts, rank, width // parts), BF),
        ],
        compiler_params=PARAMS,
    )(grad, error, left, left_t)


def inner_kernel(right_ref, basis_ref, *refs):
    outside, (inner_ref, used_ref) = refs[:-2], refs[-2:]
    group = outside[0].shape[0]

    def total(piece):
        acc = None
        for i in range(right_ref.shape[0]):
            right = piece(i)
            used_ref[i] = right
            term = dot(right, basis_ref[i])
            acc = term if acc is None else acc + term
        inner_ref[...] = acc.astype(BF)

    first = lax.axis_index("section") == 0

    @pl.when(first)
    def _():
        total(lambda i: outside[i // group][i % group])

    @pl.when(jnp.logical_not(first))
    def _():
        total(lambda i: right_ref[i])


def inner_of(right, basis, outside):
    return pl.pallas_call(
        inner_kernel,
        out_shape=[
            jax.ShapeDtypeStruct((right.shape[1], basis.shape[2]), BF),
            jax.ShapeDtypeStruct(right.shape, BF),
        ],
        compiler_params=PARAMS,
    )(right, basis, *outside)


def core_kernel(x_ref, left_t_ref, outside_ref, out_ref):
    last = lax.axis_index("section") == lax.axis_size("section") - 1
    left_t = jnp.where(last, outside_ref[...].astype(F32), left_t_ref[...].astype(F32)).astype(BF)
    core = dot(left_t, x_ref[...]).astype(BF)
    count, _, part = out_ref.shape
    for i in range(count):
        out_ref[i] = core[:, i * part : (i + 1) * part]


def core_of(inputs, left_t, outside_left_t, parts):
    _, rows, width = inputs.shape
    rank = left_t.shape[0]
    steps = parts // 2
    small = pl.BlockSpec((rank, rows), lambda m: (0, 0))
    return pl.pallas_call(
        core_kernel,
        grid=(steps,),
        in_specs=[pl.BlockSpec((None, rows, width // steps), lambda m: (0, 0, m)), small, small],
        out_specs=pl.BlockSpec((2, rank, width // parts), lambda m: (m, 0, 0)),
        out_shape=jax.ShapeDtypeStruct((parts, rank, width // parts), BF),
        compiler_params=PARAMS,
    )(inputs, left_t, outside_left_t)


def three_parts(value):
    high = value.astype(BF).astype(F32)
    value = value - high
    middle = value.astype(BF).astype(F32)
    return high, middle, (value - middle).astype(BF).astype(F32)


def sum_kernel(cores_ref, inner_ref, left_sum_ref, message_ref):
    count, rank, part = cores_ref.shape
    cores_t = cores_ref[...].reshape(count * rank, part)
    inner = inner_ref[...].reshape(count * rank, -1)
    left_sum = dot(inner, cores_t, TN)
    left_sum_ref[...] = left_sum
    high = left_sum.astype(BF)
    low = (left_sum - high.astype(F32)).astype(BF)
    mid = (dot(cores_t, high, NT) + dot(cores_t, low, NT)).astype(BF)
    gram = dot(left_sum, left_sum, NT, HIGHEST)
    share = gram.shape[0] // count
    for i in range(count):
        high, middle, low = three_parts(gram[i * share : (i + 1) * share])
        message_ref[i, :rank] = mid[i * rank : (i + 1) * rank]
        message_ref[i, rank : rank + 16] = jnp.concatenate([high, middle]).astype(BF)
        message_ref[i, rank + 16 :] = jnp.concatenate([low, jnp.zeros_like(low)]).astype(BF)


def local_sum(cores, inner):
    count, rank, part = cores.shape
    extra = inner.shape[2]
    return pl.pallas_call(
        sum_kernel,
        out_shape=[
            jax.ShapeDtypeStruct((extra, part), F32),
            jax.ShapeDtypeStruct((count, rank + 32, extra), BF),
        ],
        compiler_params=PARAMS,
    )(cores, inner)


def reduce_kernel(received_ref, mid_ref, gram_ref):
    count, rows, _ = received_ref.shape
    rank = rows - 32
    total = received_ref[0].astype(F32)
    for i in range(1, count):
        total += received_ref[i].astype(F32)
    mid_ref[...] = total[:rank].astype(BF)
    gram = total[rank : rank + 8] + total[rank + 8 : rank + 16] + total[rank + 16 : rank + 24]
    for i in range(count):
        gram_ref[i] = gram


def reduced(received):
    count, rows, extra = received.shape
    return pl.pallas_call(
        reduce_kernel,
        out_shape=[
            jax.ShapeDtypeStruct((rows - 32, extra), BF),
            jax.ShapeDtypeStruct((count, extra // count, extra), F32),
        ],
        compiler_params=PARAMS,
    )(received)


def left_kernel(left_sum_ref, gram_ref, left_ref, inverse_ref):
    extra = left_sum_ref.shape[0]
    inverse = inverse_factor(gram_ref[...].reshape(extra, extra))
    inverse_ref[...] = inverse
    left = lax.dot_general(
        left_sum_ref[...],
        inverse,
        (((0,), (1,)), ((), ())),
        precision=HIGHEST,
        preferred_element_type=F32,
    )
    left_ref[...] = left.astype(BF)


def weight_left_of(left_sum, gram):
    extra, part = left_sum.shape
    return pl.pallas_call(
        left_kernel,
        out_shape=[
            jax.ShapeDtypeStruct((part, extra), BF),
            jax.ShapeDtypeStruct((extra, extra), F32),
        ],
        compiler_params=PARAMS,
    )(left_sum, gram)


def product_kernel(right_ref, mids_ref, out_ref):
    count, rank, part = right_ref.shape
    right = right_ref[...].reshape(count * rank, part)
    out_ref[...] = dot(right, mids_ref[...].reshape(count * rank, -1), TN).astype(out_ref.dtype)


def product_of(rights, mids):
    return pl.pallas_call(
        product_kernel,
        out_shape=jax.ShapeDtypeStruct((rights.shape[2], mids.shape[2]), F32),
        compiler_params=PARAMS,
    )(rights, mids)


def scale_kernel(product_ref, inverse_ref, out_ref):
    out_ref[...] = dot(product_ref[...], inverse_ref[...], NT, HIGHEST).astype(BF)


def weight_right_of(product, inverse):
    return pl.pallas_call(
        scale_kernel,
        out_shape=jax.ShapeDtypeStruct(product.shape, BF),
        compiler_params=PARAMS,
    )(product, inverse)


def gather_by_chip(value):
    size = lax.axis_size("dp")
    pieces = [value]
    for m in range(1, size // 2):
        pieces.append(lax.ppermute(value, "dp", [(d, d ^ (2 * m)) for d in range(size)]))
    own = jnp.stack(pieces)
    return own, lax.ppermute(own, "dp", [(d, d ^ 1) for d in range(size)])


def gather_to_first(value):
    size = lax.axis_size("section")
    step = size // 4
    pieces = [value]
    for t in range(1, step):
        pieces.append(
            lax.ppermute(value, "section", [(s + t, s) for s in range(0, size, step)])
        )
    group = jnp.stack(pieces)
    groups = [group]
    for u in range(1, 4):
        groups.append(lax.ppermute(group, "section", [(u * step, 0)]))
    return groups


def spread(value):
    copies = jnp.broadcast_to(value[None], (lax.axis_size("dp"),) + value.shape)
    return lax.all_to_all(copies, "dp", 0, 0)


def after(value, *others):
    return lax.optimization_barrier((value, *others))[0]


def body(
    section_input, boundary_grad, carry_error, act_basis, weight_basis, outside_left, outside_right
):
    sections, parts = lax.axis_size("section"), lax.axis_size("dp")
    down = [(s, (s - 1) % sections) for s in range(sections)]
    up = [(s, (s + 1) % sections) for s in range(sections)]
    me = lax.axis_index("dp").astype(jnp.int32).reshape(1)

    basis_w = lax.ppermute(weight_basis[0], "section", up)
    own, other = gather_by_chip(act_basis[0].T)
    basis_w = lax.all_gather(basis_w, "dp", axis=0)
    groups = gather_to_first(outside_right[0].T)

    left, left_t = act_left(me, boundary_grad, carry_error, after(own, groups[0]), other)
    recv_left = lax.ppermute(left_t, "section", down)
    new_error, right = act_right(boundary_grad, carry_error, left, left_t, parts)
    cores = core_of(section_input, recv_left, outside_left.T, parts)
    cores = lax.all_to_all(cores, "dp", 0, 0)

    inner, rights = inner_of(right, basis_w, groups)
    inner = spread(lax.ppermute(inner, "section", down))
    rights = lax.all_to_all(after(rights, cores, inner), "dp", 0, 0)

    left_sum, message = local_sum(cores, inner)
    mid, gram = reduced(lax.all_to_all(message, "dp", 0, 0))
    gram = lax.all_to_all(gram, "dp", 0, 0)
    mids = spread(lax.ppermute(mid, "section", up))
    weight_left, inverse = weight_left_of(left_sum, gram)
    product = lax.ppermute(product_of(rights, mids), "section", down)
    weight_right = weight_right_of(product, inverse)
    return (new_error, weight_left[None], weight_right[None])


def solution(mesh):
    return jax.shard_map(
        body,
        mesh=mesh,
        in_specs=(
            P("section", "dp", None),
            P("section", "dp", None),
            P("section", "dp", None),
            P("section", "dp", None),
            P("section", "dp", None),
            P("dp", None),
            P("dp", "section", None),
        ),
        out_specs=(P("section", "dp", None), P("section", "dp", None), P("section", "dp", None)),
        check_vma=False,
    )
```

```python
import functools

import jax
import jax.numpy as jnp
from jax import lax
from jax.experimental import pallas as pl
from jax.experimental.pallas import tpu as pltpu
from jax.sharding import PartitionSpec as P

BF = jnp.bfloat16
F32 = jnp.float32
HIGHEST = lax.Precision.HIGHEST
VMEM_LIMIT = 20 * 1024 * 1024
PARAMS = pltpu.CompilerParams(vmem_limit_bytes=VMEM_LIMIT)
NN = (((1,), (0,)), ((), ()))
NT = (((1,), (1,)), ((), ()))
TN = (((0,), (0,)), ((), ()))


def dot(a, b, dims=NN, precision=None):
    return lax.dot_general(a, b, dims, precision=precision, preferred_element_type=F32)


def inverse_factor(gram):
    n = gram.shape[0]
    lane = lax.broadcasted_iota(jnp.int32, (8, n), 1)
    sub = lax.broadcasted_iota(jnp.int32, (8, n), 0)
    blocks = [gram[first : first + 8] for first in range(0, n, 8)]
    for b in range(n // 8):
        first = 8 * b
        here = (lane >= first) & (lane < first + 8)

        def spread_columns(block):
            return [jnp.broadcast_to(block[:, k : k + 1], (8, n)) for k in range(first, first + 8)]

        columns = {j: spread_columns(blocks[j]) for j in range(b, n // 8)}
        values = {j: jnp.where(here, 0.0, blocks[j]) for j in columns}
        for r in range(8):
            own = columns[b]
            scale = jnp.broadcast_to(lax.rsqrt(own[r][r : r + 1, :]), (8, n))
            pivot_row = jnp.broadcast_to(values[b][r : r + 1, :], (8, n))
            row = jnp.where(lane == first + r, 1.0, pivot_row) * scale
            scaled = own[r] * scale
            below = jnp.where(sub > r, scaled, 0.0)
            factors = [jnp.broadcast_to(scaled[q : q + 1, :], (8, n)) for q in range(r + 1, 8)]
            for j in columns:
                column = below if j == b else columns[j][r] * scale
                values[j] = values[j] - column * row
                for q in range(r + 1, 8):
                    columns[j][q] = columns[j][q] - column * factors[q - r - 1]
            values[b] = jnp.where(sub == r, row, values[b])
        for j in columns:
            blocks[j] = values[j]
    full = jnp.concatenate(blocks, axis=0)
    rows = lax.broadcasted_iota(jnp.int32, (n, n), 0)
    columns = lax.broadcasted_iota(jnp.int32, (n, n), 1)
    return jnp.where(columns <= rows, full, 0.0)


def columns_of(chip, number, width):
    return pl.ds(pl.multiple_of((chip * 2 + number) * width, width), width)


def first_kernel(g_ref, e_ref, *refs):
    blocks, out_ref = refs[:-1], refs[-1]
    device = lax.axis_index("dp")
    chip, core = device // 2, lax.rem(device, 2)
    proj = None
    for m, block_ref in enumerate(blocks):
        where = columns_of(chip ^ m, core, block_ref.shape[1])
        block = block_ref[...]
        term = dot(g_ref[0, :, where], block, NT) + dot(e_ref[0, :, where], block, NT)
        proj = term if proj is None else proj + term
    out_ref[...] = proj


def first_terms(grad, error, blocks):
    return pl.pallas_call(
        first_kernel,
        out_shape=jax.ShapeDtypeStruct((grad.shape[1], blocks[0].shape[0]), F32),
        compiler_params=PARAMS,
    )(grad, error, *blocks)


def proj_kernel(done, g_ref, e_ref, part_ref, own_ref, other_ref, left_ref, left_t_ref):
    device = lax.axis_index("dp")
    chip, core = device // 2, lax.rem(device, 2)
    pieces, _, width = own_ref.shape
    proj = part_ref[...]
    for block_ref, number, start in ((own_ref, core, done), (other_ref, 1 - core, 0)):
        for m in range(start, pieces):
            where = columns_of(chip ^ m, number, width)
            block = block_ref[m]
            proj += dot(g_ref[0, :, where], block, NT) + dot(e_ref[0, :, where], block, NT)
    inverse = inverse_factor(dot(proj, proj, TN, HIGHEST))
    left = dot(proj, inverse, NT, HIGHEST)
    left_ref[...] = left.astype(BF)
    left_t_ref[...] = left.T.astype(BF)


def act_left(grad, error, part, done, own, other):
    rows, rank = grad.shape[1], own.shape[1]
    return pl.pallas_call(
        functools.partial(proj_kernel, done),
        out_shape=[jax.ShapeDtypeStruct((rows, rank), BF), jax.ShapeDtypeStruct((rank, rows), BF)],
        compiler_params=PARAMS,
    )(grad, error, part, own, other)


def right_kernel(g_ref, e_ref, left_ref, left_t_ref, error_ref, right_ref):
    g, e = g_ref[...], e_ref[...]
    left_t = left_t_ref[...]
    right = (dot(left_t, g) + dot(left_t, e)).astype(BF)
    rebuilt = dot(left_ref[...], right)
    error_ref[...] = (g.astype(F32) + e.astype(F32) - rebuilt).astype(BF)
    part = right_ref.shape[2]
    for i in range(right_ref.shape[0]):
        right_ref[i] = right[:, i * part : (i + 1) * part]


def act_right(grad, error, left, left_t, parts):
    _, rows, width = grad.shape
    rank = left_t.shape[0]
    steps = parts // 2
    wide = pl.BlockSpec((None, rows, width // steps), lambda m: (0, 0, m))
    return pl.pallas_call(
        right_kernel,
        grid=(steps,),
        in_specs=[
            wide,
            wide,
            pl.BlockSpec((rows, rank), lambda m: (0, 0)),
            pl.BlockSpec((rank, rows), lambda m: (0, 0)),
        ],
        out_specs=[wide, pl.BlockSpec((2, rank, width // parts), lambda m: (m, 0, 0))],
        out_shape=[
            jax.ShapeDtypeStruct(grad.shape, BF),
            jax.ShapeDtypeStruct((parts, rank, width // parts), BF),
        ],
        compiler_params=PARAMS,
    )(grad, error, left, left_t)


def core_kernel(x_ref, left_t_ref, outside_ref, out_ref):
    last = lax.axis_index("section") == lax.axis_size("section") - 1
    left_t = jnp.where(last, outside_ref[...].astype(F32), left_t_ref[...].astype(F32)).astype(BF)
    core = dot(left_t, x_ref[...]).astype(BF)
    count, _, part = out_ref.shape
    for i in range(count):
        out_ref[i] = core[:, i * part : (i + 1) * part]


def core_of(inputs, left_t, outside_left_t, parts):
    _, rows, width = inputs.shape
    rank = left_t.shape[0]
    steps = parts // 2
    small = pl.BlockSpec((rank, rows), lambda m: (0, 0))
    return pl.pallas_call(
        core_kernel,
        grid=(steps,),
        in_specs=[pl.BlockSpec((None, rows, width // steps), lambda m: (0, 0, m)), small, small],
        out_specs=pl.BlockSpec((2, rank, width // parts), lambda m: (m, 0, 0)),
        out_shape=jax.ShapeDtypeStruct((parts, rank, width // parts), BF),
        compiler_params=PARAMS,
    )(inputs, left_t, outside_left_t)


def inner_kernel(right_ref, basis_ref, *refs):
    beyond, (inner_ref, message_ref, acc) = refs[:-3], refs[-3:]
    step = pl.program_id(0)
    first = lax.axis_index("section") == 0
    part = right_ref.shape[2]

    @pl.when(step == 0)
    def _():
        acc[...] = jnp.zeros_like(acc)

    def add(blocks_ref):
        term = dot(blocks_ref[0], basis_ref[0])
        for i in range(1, blocks_ref.shape[0]):
            term += dot(blocks_ref[i], basis_ref[i])
        acc[...] += term
        message_ref[:, :, :part] = blocks_ref[...]

    @pl.when(jnp.logical_not(first))
    def _():
        add(right_ref)

    for u, group in enumerate(beyond):

        @pl.when(first & (step == u))
        def _():
            add(group)

    @pl.when(step == pl.num_programs(0) - 1)
    def _():
        inner_ref[...] = acc[...].astype(BF)


def inner_of(right, basis, beyond):
    parts, rank, part = right.shape
    extra = basis.shape[2]
    steps = len(beyond)
    blocks = parts // steps
    return pl.pallas_call(
        inner_kernel,
        grid=(steps,),
        in_specs=[
            pl.BlockSpec((blocks, rank, part), lambda m: (m, 0, 0)),
            pl.BlockSpec((blocks, part, extra), lambda m: (m, 0, 0)),
        ]
        + [pl.BlockSpec(group.shape, lambda m: (0, 0, 0)) for group in beyond],
        out_specs=[
            pl.BlockSpec((rank, extra), lambda m: (0, 0)),
            pl.BlockSpec((blocks, rank, part + extra), lambda m: (m, 0, 0)),
        ],
        out_shape=[
            jax.ShapeDtypeStruct((rank, extra), BF),
            jax.ShapeDtypeStruct((parts, rank, part + extra), BF),
        ],
        scratch_shapes=[pltpu.VMEM((rank, extra), F32)],
        compiler_params=PARAMS,
    )(right, *(pltpu.with_memory_space_constraint(x, pltpu.HBM) for x in (basis, *beyond)))


def place_kernel(inner_ref, _, out_ref, sems):
    parts, _, columns = out_ref.shape
    extra = inner_ref.shape[1]
    copies = [
        pltpu.make_async_copy(
            inner_ref, out_ref.at[i, :, pl.ds(columns - extra, extra)], sems.at[i]
        )
        for i in range(parts)
    ]
    for copy in copies:
        copy.start()
    for copy in copies:
        copy.wait()


def with_inner(message, inner):
    return pl.pallas_call(
        place_kernel,
        in_specs=[pl.BlockSpec(memory_space=pltpu.VMEM), pl.BlockSpec(memory_space=pl.ANY)],
        out_specs=pl.BlockSpec(memory_space=pl.ANY),
        out_shape=jax.ShapeDtypeStruct(message.shape, BF),
        scratch_shapes=[pltpu.SemaphoreType.DMA((message.shape[0],))],
        input_output_aliases={1: 0},
        compiler_params=PARAMS,
    )(inner, message)


def three_parts(value):
    high = value.astype(BF).astype(F32)
    value = value - high
    middle = value.astype(BF).astype(F32)
    return high, middle, (value - middle).astype(BF).astype(F32)


def sum_kernel(cores_ref, inner_ref, left_sum_ref, message_ref):
    count, rank, part = cores_ref.shape
    cores_t = cores_ref[...].reshape(count * rank, part)
    inner = inner_ref[...].reshape(count * rank, -1)
    left_sum = dot(inner, cores_t, TN)
    left_sum_ref[...] = left_sum
    high = left_sum.astype(BF)
    low = (left_sum - high.astype(F32)).astype(BF)
    mid = (dot(cores_t, high, NT) + dot(cores_t, low, NT)).astype(BF)
    gram = dot(left_sum, left_sum, NT, HIGHEST)
    share = gram.shape[0] // count
    for i in range(count):
        high, middle, low = three_parts(gram[i * share : (i + 1) * share])
        message_ref[i, :rank] = mid[i * rank : (i + 1) * rank]
        message_ref[i, rank : rank + 16] = jnp.concatenate([high, middle]).astype(BF)
        message_ref[i, rank + 16 :] = jnp.concatenate([low, jnp.zeros_like(low)]).astype(BF)


def local_sum(cores, received):
    count, rank, part = cores.shape
    extra = received.shape[2] - part
    return pl.pallas_call(
        sum_kernel,
        grid=(1,),
        in_specs=[
            pl.BlockSpec((count, rank, part), lambda i: (0, 0, 0)),
            pl.BlockSpec((count, rank, extra), lambda i: (0, 0, part // extra)),
        ],
        out_specs=[
            pl.BlockSpec((extra, part), lambda i: (0, 0)),
            pl.BlockSpec((count, rank + 32, extra), lambda i: (0, 0, 0)),
        ],
        out_shape=[
            jax.ShapeDtypeStruct((extra, part), F32),
            jax.ShapeDtypeStruct((count, rank + 32, extra), BF),
        ],
        compiler_params=PARAMS,
    )(cores, received)


def reduce_kernel(received_ref, mid_ref, gram_ref):
    count, rows, _ = received_ref.shape
    rank = rows - 32
    total = received_ref[0].astype(F32)
    for i in range(1, count):
        total += received_ref[i].astype(F32)
    mid_ref[...] = total[:rank].astype(BF)
    gram = total[rank : rank + 8] + total[rank + 8 : rank + 16] + total[rank + 16 : rank + 24]
    high, middle, low = three_parts(gram)
    gram_ref[:16] = jnp.concatenate([high, middle]).astype(BF)
    gram_ref[16:] = jnp.concatenate([low, jnp.zeros_like(low)]).astype(BF)


def reduced(received):
    _, rows, extra = received.shape
    return pl.pallas_call(
        reduce_kernel,
        out_shape=[
            jax.ShapeDtypeStruct((rows - 32, extra), BF),
            jax.ShapeDtypeStruct((32, extra), BF),
        ],
        compiler_params=PARAMS,
    )(received)


def copies_kernel(mid_ref, gram_ref, out_ref):
    rank = mid_ref.shape[0]
    for i in range(out_ref.shape[0]):
        out_ref[i, :rank] = mid_ref[...]
        out_ref[i, rank:] = gram_ref[...]


def copies_of(mid, gram, count):
    rows = mid.shape[0] + gram.shape[0]
    return pl.pallas_call(
        copies_kernel,
        out_shape=jax.ShapeDtypeStruct((count, rows, mid.shape[1]), BF),
        compiler_params=PARAMS,
    )(mid, gram)


def left_kernel(left_sum_ref, message_ref, left_ref, inverse_ref):
    count, rows, _ = message_ref.shape
    gram = []
    for i in range(count):
        tail = message_ref[i, rows - 32 :].astype(F32)
        gram.append(tail[:8] + tail[8:16] + tail[16:24])
    inverse = inverse_factor(jnp.concatenate(gram, axis=0))
    inverse_ref[...] = inverse
    left = lax.dot_general(
        left_sum_ref[...],
        inverse,
        (((0,), (1,)), ((), ())),
        precision=HIGHEST,
        preferred_element_type=F32,
    )
    left_ref[...] = left.astype(BF)


def weight_left_of(left_sum, message):
    extra, part = left_sum.shape
    return pl.pallas_call(
        left_kernel,
        out_shape=[
            jax.ShapeDtypeStruct((part, extra), BF),
            jax.ShapeDtypeStruct((extra, extra), F32),
        ],
        compiler_params=PARAMS,
    )(left_sum, message)


def product_kernel(message_ref, right_ref, out_ref):
    count, rank, part = right_ref.shape
    mids = message_ref[:, :rank, :].reshape(count * rank, -1)
    out_ref[...] = dot(right_ref[...].reshape(count * rank, part), mids, TN).astype(BF)


def product_of(message, received):
    count, rows, extra = message.shape
    _, rank, columns = received.shape
    part = columns - extra
    return pl.pallas_call(
        product_kernel,
        grid=(1,),
        in_specs=[
            pl.BlockSpec((count, rows, extra), lambda i: (0, 0, 0)),
            pl.BlockSpec((count, rank, part), lambda i: (0, 0, 0)),
        ],
        out_specs=pl.BlockSpec((part, extra), lambda i: (0, 0)),
        out_shape=jax.ShapeDtypeStruct((part, extra), BF),
        compiler_params=PARAMS,
    )(message, received)


def scale_kernel(product_ref, inverse_ref, out_ref):
    inverse = inverse_ref[...]
    high = inverse.astype(BF)
    low = (inverse - high.astype(F32)).astype(BF)
    product = product_ref[...]
    out_ref[...] = (dot(product, high, NT) + dot(product, low, NT)).astype(BF)


def weight_right_of(product, inverse):
    return pl.pallas_call(
        scale_kernel,
        out_shape=jax.ShapeDtypeStruct(product.shape, BF),
        compiler_params=PARAMS,
    )(product, inverse)


def to_chip(m):
    size = lax.axis_size("dp")
    return [(d, d ^ (2 * m)) for d in range(size)]


def swap_cores(value):
    return lax.ppermute(value, "dp", [(d, d ^ 1) for d in range(lax.axis_size("dp"))])


def after(value, *others):
    return lax.optimization_barrier((value, *others))[0]


def body(
    section_input, boundary_grad, carry_error, act_basis, weight_basis, outside_left, outside_right
):
    sections, parts = lax.axis_size("section"), lax.axis_size("dp")
    down = [(s, (s - 1) % sections) for s in range(sections)]
    up = [(s, (s + 1) % sections) for s in range(sections)]
    chips = parts // 2

    beyond = outside_right[0].T
    step = sections // 4
    group = jnp.stack(
        [beyond]
        + [
            lax.ppermute(beyond, "section", [(s + t, s) for s in range(0, sections, step)])
            for t in range(1, step)
        ]
    )
    basis_w = lax.ppermute(weight_basis[0], "section", up)
    basis_a = act_basis[0].T
    own = [basis_a] + [lax.ppermute(basis_a, "dp", to_chip(m)) for m in range(1, chips)]
    basis_w = lax.all_gather(after(basis_w, group, *own[1:4]), "dp", axis=0)
    groups = [group] + [lax.ppermute(group, "section", [(u * step, 0)]) for u in range(1, 4)]
    part = first_terms(after(boundary_grad, groups[1]), carry_error, own[:4])
    own, part, groups = lax.optimization_barrier((own, part, groups))
    own = jnp.stack(own)
    other = swap_cores(own)
    left, left_t = act_left(boundary_grad, carry_error, part, 4, own, other)
    recv_left = lax.ppermute(left_t, "section", down)
    cores = core_of(section_input, recv_left, outside_left.T, parts)
    new_error, right = act_right(boundary_grad, carry_error, left, left_t, parts)
    inner, message = inner_of(after(right, cores), basis_w, groups)
    cores = lax.all_to_all(cores, "dp", 0, 0)
    message = with_inner(message, lax.ppermute(inner, "section", down))
    received = lax.all_to_all(after(message, cores), "dp", 0, 0)

    left_sum, message = local_sum(cores, received)
    mid, gram = reduced(lax.all_to_all(message, "dp", 0, 0))
    mid = lax.ppermute(mid, "section", up)
    message = lax.all_to_all(copies_of(mid, gram, parts), "dp", 0, 0)
    product = lax.ppermute(product_of(message, received), "section", down)
    weight_left, inverse = weight_left_of(left_sum, message)
    weight_right = weight_right_of(product, inverse)
    return (new_error, weight_left[None], weight_right[None])


def solution(mesh):
    return jax.shard_map(
        body,
        mesh=mesh,
        in_specs=(
            P("section", "dp", None),
            P("section", "dp", None),
            P("section", "dp", None),
            P("section", "dp", None),
            P("section", "dp", None),
            P("dp", None),
            P("dp", "section", None),
        ),
        out_specs=(P("section", "dp", None), P("section", "dp", None), P("section", "dp", None)),
        check_vma=False,
    )
```

```python
import functools

import jax
import jax.numpy as jnp
from jax import lax
from jax.experimental import pallas as pl
from jax.experimental.pallas import tpu as pltpu
from jax.sharding import PartitionSpec as P

BF = jnp.bfloat16
F32 = jnp.float32
HIGHEST = lax.Precision.HIGHEST
VMEM_LIMIT = 20 * 1024 * 1024
PARAMS = pltpu.CompilerParams(vmem_limit_bytes=VMEM_LIMIT)
NN = (((1,), (0,)), ((), ()))
NT = (((1,), (1,)), ((), ()))
TN = (((0,), (0,)), ((), ()))


def dot(a, b, dims=NN, precision=None):
    return lax.dot_general(a, b, dims, precision=precision, preferred_element_type=F32)


def inverse_factor(gram):
    n = gram.shape[0]
    lane = lax.broadcasted_iota(jnp.int32, (8, n), 1)
    sub = lax.broadcasted_iota(jnp.int32, (8, n), 0)
    blocks = [gram[first : first + 8] for first in range(0, n, 8)]
    for b in range(n // 8):
        first = 8 * b
        here = (lane >= first) & (lane < first + 8)

        def spread_columns(block):
            return [jnp.broadcast_to(block[:, k : k + 1], (8, n)) for k in range(first, first + 8)]

        columns = {j: spread_columns(blocks[j]) for j in range(b, n // 8)}
        values = {j: jnp.where(here, 0.0, blocks[j]) for j in columns}
        for r in range(8):
            own = columns[b]
            scale = jnp.broadcast_to(lax.rsqrt(own[r][r : r + 1, :]), (8, n))
            pivot_row = jnp.broadcast_to(values[b][r : r + 1, :], (8, n))
            row = jnp.where(lane == first + r, 1.0, pivot_row) * scale
            scaled = own[r] * scale
            below = jnp.where(sub > r, scaled, 0.0)
            factors = [jnp.broadcast_to(scaled[q : q + 1, :], (8, n)) for q in range(r + 1, 8)]
            for j in columns:
                column = below if j == b else columns[j][r] * scale
                values[j] = values[j] - column * row
                for q in range(r + 1, 8):
                    columns[j][q] = columns[j][q] - column * factors[q - r - 1]
            values[b] = jnp.where(sub == r, row, values[b])
        for j in columns:
            blocks[j] = values[j]
    full = jnp.concatenate(blocks, axis=0)
    rows = lax.broadcasted_iota(jnp.int32, (n, n), 0)
    columns = lax.broadcasted_iota(jnp.int32, (n, n), 1)
    return jnp.where(columns <= rows, full, 0.0)


def columns_of(chip, number, width):
    return pl.ds(pl.multiple_of((chip * 2 + number) * width, width), width)


def first_kernel(g_ref, e_ref, *refs):
    blocks, out_ref = refs[:-1], refs[-1]
    device = lax.axis_index("dp")
    chip, core = device // 2, lax.rem(device, 2)
    proj = None
    for m, block_ref in enumerate(blocks):
        where = columns_of(chip ^ m, core, block_ref.shape[1])
        block = block_ref[...]
        term = dot(g_ref[0, :, where], block, NT) + dot(e_ref[0, :, where], block, NT)
        proj = term if proj is None else proj + term
    out_ref[...] = proj


def first_terms(grad, error, blocks):
    return pl.pallas_call(
        first_kernel,
        out_shape=jax.ShapeDtypeStruct((grad.shape[1], blocks[0].shape[0]), F32),
        compiler_params=PARAMS,
    )(grad, error, *blocks)


def proj_kernel(done, g_ref, e_ref, part_ref, own_ref, other_ref, left_ref, left_t_ref):
    device = lax.axis_index("dp")
    chip, core = device // 2, lax.rem(device, 2)
    pieces, _, width = own_ref.shape
    proj = part_ref[...]
    for block_ref, number, start in ((own_ref, core, done), (other_ref, 1 - core, 0)):
        for m in range(start, pieces):
            where = columns_of(chip ^ m, number, width)
            block = block_ref[m]
            proj += dot(g_ref[0, :, where], block, NT) + dot(e_ref[0, :, where], block, NT)
    inverse = inverse_factor(dot(proj, proj, TN, HIGHEST))
    left = dot(proj, inverse, NT, HIGHEST)
    left_ref[...] = left.astype(BF)
    left_t_ref[...] = left.T.astype(BF)


def act_left(grad, error, part, done, own, other):
    rows, rank = grad.shape[1], own.shape[1]
    return pl.pallas_call(
        functools.partial(proj_kernel, done),
        out_shape=[jax.ShapeDtypeStruct((rows, rank), BF), jax.ShapeDtypeStruct((rank, rows), BF)],
        compiler_params=PARAMS,
    )(grad, error, part, own, other)


def right_kernel(g_ref, e_ref, left_ref, left_t_ref, error_ref, right_ref):
    g, e = g_ref[...], e_ref[...]
    left_t = left_t_ref[...]
    right = (dot(left_t, g) + dot(left_t, e)).astype(BF)
    rebuilt = dot(left_ref[...], right)
    error_ref[...] = (g.astype(F32) + e.astype(F32) - rebuilt).astype(BF)
    part = right_ref.shape[2]
    for i in range(right_ref.shape[0]):
        right_ref[i] = right[:, i * part : (i + 1) * part]


def act_right(grad, error, left, left_t, parts):
    _, rows, width = grad.shape
    rank = left_t.shape[0]
    steps = parts // 2
    wide = pl.BlockSpec((None, rows, width // steps), lambda m: (0, 0, m))
    return pl.pallas_call(
        right_kernel,
        grid=(steps,),
        in_specs=[
            wide,
            wide,
            pl.BlockSpec((rows, rank), lambda m: (0, 0)),
            pl.BlockSpec((rank, rows), lambda m: (0, 0)),
        ],
        out_specs=[wide, pl.BlockSpec((2, rank, width // parts), lambda m: (m, 0, 0))],
        out_shape=[
            jax.ShapeDtypeStruct(grad.shape, BF),
            jax.ShapeDtypeStruct((parts, rank, width // parts), BF),
        ],
        compiler_params=PARAMS,
    )(grad, error, left, left_t)


def core_kernel(x_ref, left_t_ref, outside_ref, out_ref, blocks, sems):
    last = lax.axis_index("section") == lax.axis_size("section") - 1
    left_t = jnp.where(last, outside_ref[...].astype(F32), left_t_ref[...].astype(F32)).astype(BF)
    count, _, part = out_ref.shape
    copies = []
    for i in range(count):
        blocks[i] = dot(left_t, x_ref[0, :, i * part : (i + 1) * part]).astype(BF)
        copies.append(pltpu.make_async_copy(blocks.at[i], out_ref.at[i], sems.at[i]))
        copies[-1].start()
    for copy in copies:
        copy.wait()


def core_of(inputs, left_t, outside_left_t, parts):
    _, _, width = inputs.shape
    shape = (parts, left_t.shape[0], width // parts)
    return pl.pallas_call(
        core_kernel,
        in_specs=[pl.BlockSpec(memory_space=pltpu.VMEM)] * 3,
        out_specs=pl.BlockSpec(memory_space=pltpu.HBM),
        out_shape=jax.ShapeDtypeStruct(shape, BF),
        scratch_shapes=[pltpu.VMEM(shape, BF), pltpu.SemaphoreType.DMA((parts,))],
        compiler_params=PARAMS,
    )(inputs, left_t, outside_left_t)


def inner_kernel(right_ref, basis_ref, *refs):
    beyond, (inner_ref, message_ref, acc) = refs[:-3], refs[-3:]
    step = pl.program_id(0)
    first = lax.axis_index("section") == 0
    part = right_ref.shape[2]

    @pl.when(step == 0)
    def _():
        acc[...] = jnp.zeros_like(acc)

    def add(blocks_ref):
        term = dot(blocks_ref[0], basis_ref[0])
        for i in range(1, blocks_ref.shape[0]):
            term += dot(blocks_ref[i], basis_ref[i])
        acc[...] += term
        message_ref[:, :, :part] = blocks_ref[...]

    @pl.when(jnp.logical_not(first))
    def _():
        add(right_ref)

    for u, group in enumerate(beyond):

        @pl.when(first & (step == u))
        def _():
            add(group)

    @pl.when(step == pl.num_programs(0) - 1)
    def _():
        inner_ref[...] = acc[...].astype(BF)


def inner_of(right, basis, beyond):
    parts, rank, part = right.shape
    extra = basis.shape[2]
    steps = len(beyond)
    blocks = parts // steps
    return pl.pallas_call(
        inner_kernel,
        grid=(steps,),
        in_specs=[
            pl.BlockSpec((blocks, rank, part), lambda m: (m, 0, 0)),
            pl.BlockSpec((blocks, part, extra), lambda m: (m, 0, 0)),
        ]
        + [pl.BlockSpec(group.shape, lambda m: (0, 0, 0)) for group in beyond],
        out_specs=[
            pl.BlockSpec((rank, extra), lambda m: (0, 0)),
            pl.BlockSpec((blocks, rank, part + extra), lambda m: (m, 0, 0)),
        ],
        out_shape=[
            jax.ShapeDtypeStruct((rank, extra), BF),
            jax.ShapeDtypeStruct((parts, rank, part + extra), BF),
        ],
        scratch_shapes=[pltpu.VMEM((rank, extra), F32)],
        compiler_params=PARAMS,
    )(right, *(pltpu.with_memory_space_constraint(x, pltpu.HBM) for x in (basis, *beyond)))


def place_kernel(inner_ref, _, out_ref, sems):
    parts, _, columns = out_ref.shape
    extra = inner_ref.shape[1]
    copies = [
        pltpu.make_async_copy(
            inner_ref, out_ref.at[i, :, pl.ds(columns - extra, extra)], sems.at[i]
        )
        for i in range(parts)
    ]
    for copy in copies:
        copy.start()
    for copy in copies:
        copy.wait()


def with_inner(message, inner):
    return pl.pallas_call(
        place_kernel,
        in_specs=[pl.BlockSpec(memory_space=pltpu.VMEM), pl.BlockSpec(memory_space=pl.ANY)],
        out_specs=pl.BlockSpec(memory_space=pl.ANY),
        out_shape=jax.ShapeDtypeStruct(message.shape, BF),
        scratch_shapes=[pltpu.SemaphoreType.DMA((message.shape[0],))],
        input_output_aliases={1: 0},
        compiler_params=PARAMS,
    )(inner, message)


def three_parts(value):
    high = value.astype(BF).astype(F32)
    value = value - high
    middle = value.astype(BF).astype(F32)
    return high, middle, (value - middle).astype(BF).astype(F32)


def sum_kernel(cores_ref, inner_ref, left_sum_ref, message_ref, cores, sems):
    count, rank, part = cores_ref.shape
    groups = sems.shape[0]
    each = count // groups
    copies = []
    for i in range(groups):
        where = pl.ds(i * each, each)
        copies.append(pltpu.make_async_copy(cores_ref.at[where], cores.at[where], sems.at[i]))
        copies[-1].start()
    left_sum = None
    for i, copy in enumerate(copies):
        copy.wait()
        block = cores[i * each : (i + 1) * each].reshape(each * rank, part)
        inner = inner_ref[i * each : (i + 1) * each].reshape(each * rank, -1)
        term = dot(inner, block, TN)
        left_sum = term if left_sum is None else left_sum + term
    cores_t = cores[...].reshape(count * rank, part)
    left_sum_ref[...] = left_sum
    high = left_sum.astype(BF)
    low = (left_sum - high.astype(F32)).astype(BF)
    mid = (dot(cores_t, high, NT) + dot(cores_t, low, NT)).astype(BF)
    gram = dot(left_sum, left_sum, NT, HIGHEST)
    share = gram.shape[0] // count
    for i in range(count):
        high, middle, low = three_parts(gram[i * share : (i + 1) * share])
        message_ref[i, :rank] = mid[i * rank : (i + 1) * rank]
        message_ref[i, rank : rank + 16] = jnp.concatenate([high, middle]).astype(BF)
        message_ref[i, rank + 16 :] = jnp.concatenate([low, jnp.zeros_like(low)]).astype(BF)


def local_sum(cores, received):
    count, rank, part = cores.shape
    extra = received.shape[2] - part
    return pl.pallas_call(
        sum_kernel,
        grid=(1,),
        in_specs=[
            pl.BlockSpec(memory_space=pltpu.HBM),
            pl.BlockSpec((count, rank, extra), lambda i: (0, 0, part // extra)),
        ],
        out_specs=[
            pl.BlockSpec((extra, part), lambda i: (0, 0)),
            pl.BlockSpec((count, rank + 32, extra), lambda i: (0, 0, 0)),
        ],
        out_shape=[
            jax.ShapeDtypeStruct((extra, part), F32),
            jax.ShapeDtypeStruct((count, rank + 32, extra), BF),
        ],
        scratch_shapes=[pltpu.VMEM(cores.shape, BF), pltpu.SemaphoreType.DMA((4,))],
        compiler_params=PARAMS,
    )(cores, received)


def reduce_kernel(received_ref, mid_ref, gram_ref):
    count, rows, _ = received_ref.shape
    rank = rows - 32
    total = received_ref[0].astype(F32)
    for i in range(1, count):
        total += received_ref[i].astype(F32)
    mid_ref[...] = total[:rank].astype(BF)
    gram = total[rank : rank + 8] + total[rank + 8 : rank + 16] + total[rank + 16 : rank + 24]
    high, middle, low = three_parts(gram)
    gram_ref[:16] = jnp.concatenate([high, middle]).astype(BF)
    gram_ref[16:] = jnp.concatenate([low, jnp.zeros_like(low)]).astype(BF)


def reduced(received):
    _, rows, extra = received.shape
    return pl.pallas_call(
        reduce_kernel,
        out_shape=[
            jax.ShapeDtypeStruct((rows - 32, extra), BF),
            jax.ShapeDtypeStruct((32, extra), BF),
        ],
        compiler_params=PARAMS,
    )(received)


def copies_kernel(mid_ref, gram_ref, out_ref):
    rank = mid_ref.shape[0]
    for i in range(out_ref.shape[0]):
        out_ref[i, :rank] = mid_ref[...]
        out_ref[i, rank:] = gram_ref[...]


def copies_of(mid, gram, count):
    rows = mid.shape[0] + gram.shape[0]
    return pl.pallas_call(
        copies_kernel,
        out_shape=jax.ShapeDtypeStruct((count, rows, mid.shape[1]), BF),
        compiler_params=PARAMS,
    )(mid, gram)


def left_kernel(left_sum_ref, message_ref, left_ref, inverse_ref):
    count, rows, _ = message_ref.shape
    gram = []
    for i in range(count):
        tail = message_ref[i, rows - 32 :].astype(F32)
        gram.append(tail[:8] + tail[8:16] + tail[16:24])
    inverse = inverse_factor(jnp.concatenate(gram, axis=0))
    inverse_ref[...] = inverse
    left = lax.dot_general(
        left_sum_ref[...],
        inverse,
        (((0,), (1,)), ((), ())),
        precision=HIGHEST,
        preferred_element_type=F32,
    )
    left_ref[...] = left.astype(BF)


def weight_left_of(left_sum, message):
    extra, part = left_sum.shape
    return pl.pallas_call(
        left_kernel,
        out_shape=[
            jax.ShapeDtypeStruct((part, extra), BF),
            jax.ShapeDtypeStruct((extra, extra), F32),
        ],
        compiler_params=PARAMS,
    )(left_sum, message)


def product_kernel(message_ref, right_ref, out_ref):
    count, rank, part = right_ref.shape
    mids = message_ref[:, :rank, :].reshape(count * rank, -1)
    out_ref[...] = dot(right_ref[...].reshape(count * rank, part), mids, TN).astype(BF)


def product_of(message, received):
    count, rows, extra = message.shape
    _, rank, columns = received.shape
    part = columns - extra
    return pl.pallas_call(
        product_kernel,
        grid=(1,),
        in_specs=[
            pl.BlockSpec((count, rows, extra), lambda i: (0, 0, 0)),
            pl.BlockSpec((count, rank, part), lambda i: (0, 0, 0)),
        ],
        out_specs=pl.BlockSpec((part, extra), lambda i: (0, 0)),
        out_shape=jax.ShapeDtypeStruct((part, extra), BF),
        compiler_params=PARAMS,
    )(message, received)


def scale_kernel(product_ref, inverse_ref, out_ref):
    inverse = inverse_ref[...]
    high = inverse.astype(BF)
    low = (inverse - high.astype(F32)).astype(BF)
    product = product_ref[...]
    out_ref[...] = (dot(product, high, NT) + dot(product, low, NT)).astype(BF)


def weight_right_of(product, inverse):
    return pl.pallas_call(
        scale_kernel,
        out_shape=jax.ShapeDtypeStruct(product.shape, BF),
        compiler_params=PARAMS,
    )(product, inverse)


def to_chip(m):
    size = lax.axis_size("dp")
    return [(d, d ^ (2 * m)) for d in range(size)]


def swap_cores(value):
    return lax.ppermute(value, "dp", [(d, d ^ 1) for d in range(lax.axis_size("dp"))])


def after(value, *others):
    return lax.optimization_barrier((value, *others))[0]


def body(
    section_input, boundary_grad, carry_error, act_basis, weight_basis, outside_left, outside_right
):
    sections, parts = lax.axis_size("section"), lax.axis_size("dp")
    down = [(s, (s - 1) % sections) for s in range(sections)]
    up = [(s, (s + 1) % sections) for s in range(sections)]
    chips = parts // 2

    beyond = outside_right[0].T
    step = sections // 4
    group = jnp.stack(
        [beyond]
        + [
            lax.ppermute(beyond, "section", [(s + t, s) for s in range(0, sections, step)])
            for t in range(1, step)
        ]
    )
    basis_w = lax.ppermute(weight_basis[0], "section", up)
    basis_a = act_basis[0].T
    own = [basis_a] + [lax.ppermute(basis_a, "dp", to_chip(m)) for m in range(1, chips)]
    basis_w = lax.all_gather(after(basis_w, group, *own[1:4]), "dp", axis=0)
    groups = [group] + [lax.ppermute(group, "section", [(u * step, 0)]) for u in range(1, 4)]
    part = first_terms(after(boundary_grad, groups[1]), carry_error, own[:4])
    own, part, groups = lax.optimization_barrier((own, part, groups))
    own = jnp.stack(own)
    other = swap_cores(own)
    left, left_t = act_left(boundary_grad, carry_error, part, 4, own, other)
    recv_left = lax.ppermute(left_t, "section", down)
    cores = core_of(section_input, recv_left, outside_left.T, parts)
    new_error, right = act_right(boundary_grad, carry_error, left, left_t, parts)
    inner, message = inner_of(after(right, cores), basis_w, groups)
    cores = lax.all_to_all(cores, "dp", 0, 0)
    message = with_inner(message, lax.ppermute(inner, "section", down))
    received = lax.all_to_all(after(message, cores), "dp", 0, 0)

    left_sum, message = local_sum(cores, received)
    mid, gram = reduced(lax.all_to_all(message, "dp", 0, 0))
    mid = lax.ppermute(mid, "section", up)
    message = lax.all_to_all(copies_of(mid, gram, parts), "dp", 0, 0)
    product = lax.ppermute(product_of(message, received), "section", down)
    weight_left, inverse = weight_left_of(left_sum, message)
    weight_right = weight_right_of(product, inverse)
    return (new_error, weight_left[None], weight_right[None])


def solution(mesh):
    return jax.shard_map(
        body,
        mesh=mesh,
        in_specs=(
            P("section", "dp", None),
            P("section", "dp", None),
            P("section", "dp", None),
            P("section", "dp", None),
            P("section", "dp", None),
            P("dp", None),
            P("dp", "section", None),
        ),
        out_specs=(P("section", "dp", None), P("section", "dp", None), P("section", "dp", None)),
        check_vma=False,
    )
```
